256 devices in a mesh: dp: 8 (over z_hi, y), fsdp: 32 (over z_lo, x, core).
Axes of the slice: x: 4, y: 4, z: 8 (z_hi: 2, z_lo: 4; z = z_hi * 4 + z_lo), core: 2. Of those that a mesh axis runs over, the one named last changes fastest.
Arguments:
- partial_grads: bfloat16 [8, 16, 56, 256, 256], P('dp', None, None, 'fsdp'), may hold values from -6 to 6
- owners: int32 [16, 56], replicated, may hold values from 0 to 191, as said below
- left_roots: bfloat16 [8, 192, 256, 256], P('dp', 'fsdp'), may hold values from -0.5 to 1.5, as said below
- right_roots: bfloat16 [8, 192, 256, 256], P('dp', 'fsdp'), may hold values from -0.5 to 1.5, as said below
- left_stats: float32 [8, 192, 256, 256], P('dp', 'fsdp'), may hold values from -1 to 4, as said below
- right_stats: float32 [8, 192, 256, 256], P('dp', 'fsdp'), may hold values from -1 to 4, as said below
Outputs:
- update: bfloat16 [16, 56, 256, 256], P(None, 'dp', 'fsdp')
- new_left_stats: float32 [8, 192, 256, 256], P('dp', 'fsdp')
- new_right_stats: float32 [8, 192, 256, 256], P('dp', 'fsdp')
The draws below stay inside these ranges and needn't reach their ends.
Inputs may be any that keep to these rules, and one draw needn't show every extreme that they name: `owners`: within the blocks of one index of dp (block columns g * 7 to (g + 1) * 7 - 1) no two blocks share a value; a value v names slot v % 6 of device v // 6 along fsdp, so each device holds at most 6 blocks of its index of dp, and in every index of dp some device holds exactly 6. `left_roots`: symmetric in the last two dimensions. `right_roots`: symmetric in the last two dimensions. `left_stats`: symmetric in the last two dimensions. `right_stats`: symmetric in the last two dimensions.
All inputs are finite; a program needn't handle non-finite values.
Results may differ from the reference program's by a relative error of at most 0.02.
Values may be sent and summed in bfloat16 or wider, within the bound.
A program may use at most 64 MiB of HBM per device.

```python
import math
import jax
import jax.numpy as jnp
from jax import lax

B = 256
BR = 16
BC = 56
BCD = 7
NBG = 112
SLOTS = 6
GSLOTS = 192
N_DP = 8
N_FSDP = 32


def symmetric_mix(diagonal, offdiag):
    shape = diagonal.shape
    on_diag = lax.broadcasted_iota(jnp.int32, shape, 2) == lax.broadcasted_iota(jnp.int32, shape, 3)
    mirrored = (offdiag + jnp.swapaxes(offdiag, 2, 3)) / math.sqrt(2.0)
    return jnp.where(on_diag, diagonal, mirrored)


def root_like(key_diag, key_off, shape):
    diagonal = jnp.exp(jax.random.uniform(key_diag, shape, jnp.float32, math.log(0.3), math.log(1.5)))
    offdiag = 0.03 * jax.random.normal(key_off, shape, jnp.float32)
    return symmetric_mix(diagonal, offdiag)


def stat_like(key_diag, key_off, shape):
    diagonal = jax.random.uniform(key_diag, shape, jnp.float32, 1.0, 4.0)
    offdiag = 0.1 * jax.random.normal(key_off, shape, jnp.float32)
    return symmetric_mix(diagonal, offdiag)


def draw_owners(key, part):
    key = jax.random.fold_in(key, 5)
    group_keys = jax.random.split(key, N_DP)

    def one_group(group_key):
        key_first, key_rest, key_order = jax.random.split(group_key, 3)
        first = jax.random.randint(key_first, (), 0, N_FSDP, dtype=jnp.int32)
        others = jnp.arange(N_FSDP - 1, dtype=jnp.int32)
        others = others + (others >= first).astype(jnp.int32)
        other_ids = (others[:, None] * SLOTS + jnp.arange(SLOTS, dtype=jnp.int32)[None, :]).reshape(-1)
        other_ids = jax.random.permutation(key_rest, other_ids)
        full_ids = first * SLOTS + jnp.arange(SLOTS, dtype=jnp.int32)
        chosen = jnp.concatenate([full_ids, other_ids[:NBG - SLOTS]])
        return jax.random.permutation(key_order, chosen)
    table = jax.vmap(one_group)(group_keys)
    table = jnp.transpose(table.reshape(N_DP, BR, BCD), (1, 0, 2)).reshape(BR, BC)
    return table.astype(jnp.int32)


def draw_left_roots(key, part):
    key = jax.random.fold_in(key, 11)
    key_diag, key_off = jax.random.split(key)
    return root_like(key_diag, key_off, (N_DP, GSLOTS, B, B)).astype(jnp.bfloat16)


def draw_right_roots(key, part):
    key = jax.random.fold_in(key, 13)
    key_diag, key_off = jax.random.split(key)
    return root_like(key_diag, key_off, (N_DP, GSLOTS, B, B)).astype(jnp.bfloat16)


def draw_left_stats(key, part):
    key = jax.random.fold_in(key, 17)
    key_diag, key_off = jax.random.split(key)
    return stat_like(key_diag, key_off, (N_DP, GSLOTS, B, B))


def draw_right_stats(key, part):
    key = jax.random.fold_in(key, 19)
    key_diag, key_off = jax.random.split(key)
    return stat_like(key_diag, key_off, (N_DP, GSLOTS, B, B))


def with_spikes(entries, key, source, target, blocks, factor):
    def block_of(axis_at):
        return (jnp.arange(entries.shape[axis_at]) // (entries.shape[axis_at] // blocks)).reshape((-1,) + (1,) * (entries.ndim - 1 - axis_at))

    first = jax.random.permutation(key, blocks)[block_of(target)]
    second = (block_of(target) + blocks // 2) % blocks
    return jnp.where((block_of(source) == first) | (block_of(source) == second), factor * entries, entries)


def levels(rng, extent, cuts, smallest, top_value):
    gain = 1.0
    for dim, blocks in cuts:
        heights = jax.random.uniform(jax.random.fold_in(jax.random.fold_in(rng, 6), dim), (blocks,), jnp.float32, smallest / len(cuts), top_value / len(cuts))
        gain = gain * jnp.repeat(jnp.exp(heights), extent[dim] // blocks).reshape((-1,) + (1,) * (len(extent) - 1 - dim))
    return gain


def bell_draw_with(stream_key, dims, spread, limit, cuts, heavy, held_as=jnp.bfloat16):
    drawn = spread * jax.random.normal(stream_key, dims, jnp.float32)
    if cuts:
        drawn = drawn * levels(stream_key, dims, cuts, -0.22, 0.18)
    return jnp.clip(with_spikes(drawn, jax.random.fold_in(stream_key, 3), *heavy), -limit, limit).astype(held_as)


def setup_inputs(seed: int = 0) -> dict:
    keys = jax.random.split(jax.random.key(seed), 7)
    return {
        "partial_grads": bell_draw_with(keys[0], (N_DP, BR, BC, B, B), 1.0, 6.0, ((0, 8), (3, 32)), (0, 2, 8, 2.0)),
        "owners": draw_owners(jax.random.fold_in(keys[6], 71), 0),
        "left_roots": draw_left_roots(jax.random.fold_in(keys[6], 71), 0),
        "right_roots": draw_right_roots(jax.random.fold_in(keys[6], 71), 0),
        "left_stats": draw_left_stats(jax.random.fold_in(keys[6], 71), 0),
        "right_stats": draw_right_stats(jax.random.fold_in(keys[6], 71), 0),
    }


decay = 0.95


def one_group(pieces):
    grad_group, slot_ids, left_root, right_root, left_stat, right_stat = pieces
    count = slot_ids.shape[0]
    holder = jnp.zeros((GSLOTS,), jnp.int32).at[slot_ids].set(jnp.arange(count, dtype=jnp.int32))
    occupied = jnp.zeros((GSLOTS,), jnp.float32).at[slot_ids].set(1.0) > 0.5
    per_slot = grad_group[holder].astype(jnp.float32)
    outer_left = jnp.einsum("sij,skj->sik", per_slot, per_slot)
    outer_right = jnp.einsum("sji,sjk->sik", per_slot, per_slot)
    keep = occupied[:, None, None]
    new_left = jnp.where(keep, decay * left_stat + (1.0 - decay) * outer_left, left_stat)
    new_right = jnp.where(keep, decay * right_stat + (1.0 - decay) * outer_right, right_stat)
    left_half = jnp.einsum("nij,njk->nik", left_root[slot_ids].astype(jnp.float32),
                           grad_group.astype(jnp.float32)).astype(jnp.bfloat16)
    update = jnp.einsum("nij,njk->nik", left_half.astype(jnp.float32),
                        right_root[slot_ids].astype(jnp.float32)).astype(jnp.bfloat16)
    return update, new_left, new_right


def reference(partial_grads, owners, left_roots, right_roots, left_stats, right_stats):
    grad_sum = jnp.sum(partial_grads, axis=0, dtype=jnp.float32)
    gradient = (grad_sum / N_DP).astype(jnp.bfloat16)
    grouped = jnp.transpose(gradient.reshape(BR, N_DP, BCD, B, B), (1, 0, 2, 3, 4)).reshape(N_DP, NBG, B, B)
    slot_table = jnp.transpose(owners.reshape(BR, N_DP, BCD), (1, 0, 2)).reshape(N_DP, NBG).astype(jnp.int32)
    updates, new_left, new_right = lax.map(one_group, (grouped, slot_table, left_roots, right_roots, left_stats, right_stats))
    update = jnp.transpose(updates.reshape(N_DP, BR, BCD, B, B), (1, 0, 2, 3, 4)).reshape(BR, BC, B, B)
    return update, new_left, new_right
```

```python
import jax
import jax.numpy as jnp
from jax import lax
from jax.experimental import pallas as pl
from jax.experimental.pallas import tpu as pltpu
from jax.sharding import PartitionSpec as P

MESH = pl.DeviceIdType.MESH
DECAY = 0.95
BR, BCD, ROWS, B = 16, 7, 8, 256
NBG, SLOTS, NF, NY, NDP = 112, 6, 32, 4, 8
HALF = B // 2
HR = BR // 2


def kernel(
    pg, inv, own, coef, lroot, rroot, lstat, rstat,
    upd, nl, nr,
    far, raw, com, mix, near, mine, part, zout, zin, grad, snd, rcv, ret, back,
    lv, rv, lsv, rsv, nlv, nrv,
    far_s, far_r, raw_s, raw_r, com_s, com_r, near_s, mine_s, z_s, z_r,
    a_s, a_r, b_s, b_r, load_s, out_s,
):
    dp = lax.axis_index("dp")
    me = lax.axis_index("fsdp")
    zh, y = dp // NY, dp % NY
    up, down = (y + 1) % NY, (y + 3) % NY
    over = (y + 2) % NY
    to = (zh * NY + up, zh * NY + down)
    across = (1 - zh) * NY + y

    barrier = pltpu.get_barrier_semaphore()
    for d in to + (across,):
        pl.semaphore_signal(barrier, inc=1, device_id={"dp": d}, device_id_type=MESH)
    for k in range(1, NF):
        pl.semaphore_signal(
            barrier, inc=1, device_id={"fsdp": (me + k) % NF}, device_id_type=MESH
        )

    units = [(c, h) for c in range(2) for h in range(2)]

    def cut(k, rows, target):
        c, h = units[k]
        side = 1 - zh if h == 0 else zh
        g = side * NY + target
        return pg.at[rows, pl.ds(g * BCD, BCD), :, pl.ds(c * HALF, HALF)]

    first, second, both = pl.ds(0, HR), pl.ds(HR, HR), pl.ds(0, BR)
    near_cp, mine_cp = {}, {}
    for k in range(4):
        near_cp[k, 0] = pltpu.make_async_copy(cut(k, first, up), near.at[k, 0], near_s.at[k, 0])
        near_cp[k, 1] = pltpu.make_async_copy(cut(k, second, down), near.at[k, 1], near_s.at[k, 1])
        mine_cp[k] = pltpu.make_async_copy(cut(k, both, y), mine.at[k], mine_s.at[k])
    loads = [
        pltpu.make_async_copy(src, dst, load_s.at[i])
        for i, (src, dst) in enumerate(((lroot, lv), (rroot, rv), (lstat, lsv), (rstat, rsv)))
    ]
    for k in range(4):
        near_cp[k, 0].start()
        near_cp[k, 1].start()
        mine_cp[k].start()

    pl.semaphore_wait(barrier, 3 + NF - 1)

    def remote(src, dst, s, r, device):
        cp = pltpu.make_async_remote_copy(
            src_ref=src, dst_ref=dst, send_sem=s, recv_sem=r, device_id=device, device_id_type=MESH
        )
        cp.start()
        return cp

    far_cp, raw_cp, com_cp, z_cp = {}, {}, {}, {}

    def send_far(k):
        for d, rows in enumerate((first, second)):
            far_cp[k, d] = remote(
                cut(k, rows, over), far.at[k, d], far_s.at[k, d], far_r.at[k, d], {"dp": to[d]}
            )

    def send_raw(k):
        for d, (rows, target) in enumerate(((second, up), (first, down))):
            raw_cp[k, d] = remote(
                cut(k, rows, target), raw.at[k, d], raw_s.at[k, d], raw_r.at[k, d], {"dp": to[d]}
            )

    def send_com(k):
        for d in range(2):
            near_cp[k, d].wait()
            far_cp[k, d].wait_recv()

            def add(r, _):
                mix[k, d, r] = far[k, d, r] + near[k, d, r]
                return 0

            lax.fori_loop(0, HR, add, 0)
            com_cp[k, d] = remote(
                mix.at[k, d], com.at[k, d], com_s.at[k, d], com_r.at[k, d], {"dp": to[d]}
            )

    def finish(k):
        c, h = units[k]
        mine_cp[k].wait()
        for d in range(2):
            raw_cp[k, d].wait_recv()
            com_cp[k, d].wait_recv()
        f32 = jnp.float32

        def add(r, _):
            for d in range(2):
                total = mine[k, d * HR + r].astype(f32) + com[k, d, r].astype(f32)
                total = total + raw[k, 1 - d, r].astype(f32)
                if h == 0:
                    zout[c, d * HR + r] = total.astype(jnp.bfloat16)
                else:
                    part[c, d * HR + r] = total
            return 0

        lax.fori_loop(0, HR, add, 0)
        if h == 0:
            z_cp[c] = remote(zout.at[c], zin.at[c], z_s.at[c], z_r.at[c], {"dp": across})

    a_cp = {}

    def exchange(c):
        z_cp[c].wait_recv()

        def add(r, _):
            total = (part[c, r] + zin[c, r].astype(jnp.float32)) / NDP
            grad[c, pl.ds(r * BCD, BCD)] = total.astype(jnp.bfloat16)
            return 0

        lax.fori_loop(0, BR, add, 0)

        def pack(i, _):
            for j in range(SLOTS):
                snd[c, i * SLOTS + j] = grad[c, inv[i * SLOTS + j]]
            return 0

        lax.fori_loop(0, NF, pack, 0)
        for k in range(1, NF):
            dst = (me + k) % NF
            a_cp[c, k] = remote(
                snd.at[c, pl.ds(dst * SLOTS, SLOTS)], rcv.at[c, me],
                a_s.at[c, k], a_r.at[c, k], {"fsdp": dst},
            )
        rcv[c, me] = snd[c, pl.ds(me * SLOTS, SLOTS)]

    send_far(0)
    send_far(1)
    send_raw(0)
    send_com(0)
    send_far(2)
    send_raw(1)
    for cp in loads:
        cp.start()
    send_com(1)
    finish(0)
    send_far(3)
    send_raw(2)
    send_com(2)
    finish(1)
    send_raw(3)
    send_com(3)
    exchange(0)
    finish(2)
    finish(3)
    exchange(1)

    for c in range(2):
        for k in range(1, NF):
            a_cp[c, k].wait_recv()
    for cp in loads:
        cp.wait()

    def block(s):
        halves = [
            rcv[c, :, s].astype(jnp.float32).reshape(B, HALF).astype(jnp.bfloat16) for c in range(2)
        ]
        return jnp.concatenate(halves, axis=1)

    b_cp = {}
    for s in range(SLOTS):
        g = block(s)
        half = jnp.dot(lv[s], g, preferred_element_type=jnp.float32).astype(jnp.bfloat16)
        u = jnp.dot(half, rv[s], preferred_element_type=jnp.float32).astype(jnp.bfloat16)
        ret[:, s] = u.astype(jnp.float32).reshape(NF, ROWS, B).astype(jnp.bfloat16)
        if s % 2 == 1:
            p = s // 2
            for k in range(1, NF):
                dst = (me + k) % NF
                b_cp[p, k] = remote(
                    ret.at[dst, pl.ds(2 * p, 2)], back.at[pl.ds(me * SLOTS + 2 * p, 2)],
                    b_s.at[p, k], b_r.at[p, k], {"fsdp": dst},
                )
            back[pl.ds(me * SLOTS + 2 * p, 2)] = ret[me, pl.ds(2 * p, 2)]

    outs = []
    for s in range(SLOTS):
        g = block(s)
        keep, gain = coef[0, s], coef[1, s]
        left = lax.dot_general(g, g, (((1,), (1,)), ((), ())), preferred_element_type=jnp.float32)
        nlv[s] = keep * lsv[s] + gain * left
        outs.append(pltpu.make_async_copy(nlv.at[s], nl.at[s], out_s.at[0, s]))
        outs[-1].start()
        right = lax.dot_general(g, g, (((0,), (0,)), ((), ())), preferred_element_type=jnp.float32)
        nrv[s] = keep * rsv[s] + gain * right
        outs.append(pltpu.make_async_copy(nrv.at[s], nr.at[s], out_s.at[1, s]))
        outs[-1].start()

    for k in range(4):
        for d in range(2):
            far_cp[k, d].wait_send()
            raw_cp[k, d].wait_send()
            com_cp[k, d].wait_send()
    for c in range(2):
        z_cp[c].wait_send()
        for k in range(1, NF):
            a_cp[c, k].wait_send()
    for p in range(SLOTS // 2):
        for k in range(1, NF):
            b_cp[p, k].wait()
    for cp in outs:
        cp.wait()

    def unpack(i, _):
        for j in range(BCD):
            upd[i, j] = back[own[i * BCD + j]]
        return 0

    lax.fori_loop(0, BR, unpack, 0)


def body(partial_grads, owners, left_roots, right_roots, left_stats, right_stats):
    dp = lax.axis_index("dp")
    me = lax.axis_index("fsdp")
    own = lax.dynamic_slice_in_dim(owners, dp * BCD, BCD, 1).reshape(-1)
    slots = jnp.arange(NF * SLOTS, dtype=jnp.int32)
    hit = slots[:, None] == own[None, :]
    inv = jnp.sum(jnp.where(hit, jnp.arange(NBG, dtype=jnp.int32)[None, :], 0), axis=1, dtype=jnp.int32)
    mine = me * SLOTS + jnp.arange(SLOTS, dtype=jnp.int32)
    occupied = jnp.any(mine[:, None] == own[None, :], axis=1)
    coef = jnp.stack(
        [jnp.where(occupied, DECAY, 1.0), jnp.where(occupied, 1.0 - DECAY, 0.0)]
    ).astype(jnp.float32)
    bf, f32 = jnp.bfloat16, jnp.float32
    any_ = pl.BlockSpec(memory_space=pl.ANY)
    smem = pl.BlockSpec(memory_space=pltpu.SMEM)
    vmem = pl.BlockSpec(memory_space=pltpu.VMEM)
    dma = pltpu.SemaphoreType.DMA
    unit = (4, 2, HR, BCD, ROWS, HALF)
    upd, nl, nr = pl.pallas_call(
        kernel,
        out_shape=(
            jax.ShapeDtypeStruct((BR, BCD, ROWS, B), bf),
            jax.ShapeDtypeStruct((SLOTS, B, B), f32),
            jax.ShapeDtypeStruct((SLOTS, B, B), f32),
        ),
        in_specs=[any_, smem, smem, smem, any_, any_, any_, any_],
        out_specs=(vmem, any_, any_),
        scratch_shapes=[
            pltpu.VMEM(unit, bf), pltpu.VMEM(unit, bf), pltpu.VMEM(unit, bf), pltpu.VMEM(unit, bf),
            pltpu.VMEM(unit, bf),
            pltpu.VMEM((4, BR, BCD, ROWS, HALF), bf),
            pltpu.VMEM((2, BR, BCD, ROWS, HALF), f32),
            pltpu.VMEM((2, BR, BCD, ROWS, HALF), bf),
            pltpu.VMEM((2, BR, BCD, ROWS, HALF), bf),
            pltpu.VMEM((2, NBG, ROWS, HALF), bf),
            pltpu.VMEM((2, NF * SLOTS, ROWS, HALF), bf),
            pltpu.VMEM((2, NF, SLOTS, ROWS, HALF), bf),
            pltpu.VMEM((NF, SLOTS, ROWS, B), bf),
            pltpu.VMEM((NF * SLOTS, ROWS, B), bf),
            pltpu.VMEM((SLOTS, B, B), bf), pltpu.VMEM((SLOTS, B, B), bf),
            pltpu.VMEM((SLOTS, B, B), f32), pltpu.VMEM((SLOTS, B, B), f32),
            pltpu.VMEM((SLOTS, B, B), f32), pltpu.VMEM((SLOTS, B, B), f32),
            dma((4, 2)), dma((4, 2)), dma((4, 2)), dma((4, 2)), dma((4, 2)), dma((4, 2)),
            dma((4, 2)), dma((4,)), dma((2,)), dma((2,)),
            dma((2, NF)), dma((2, NF)), dma((3, NF)), dma((3, NF)), dma((4,)), dma((2, SLOTS)),
        ],
        compiler_params=pltpu.CompilerParams(
            collective_id=0, has_side_effects=True, vmem_limit_bytes=48 * 2**20
        ),
        name="step",
    )(
        partial_grads[0], inv, own, coef,
        left_roots[0], right_roots[0], left_stats[0], right_stats[0],
    )
    return upd, nl[None], nr[None]


def solution(mesh):
    placed = (
        P("dp", None, None, "fsdp", None),
        P(),
        P("dp", "fsdp", None, None),
        P("dp", "fsdp", None, None),
        P("dp", "fsdp", None, None),
        P("dp", "fsdp", None, None),
    )
    return jax.shard_map(
        body,
        mesh=mesh,
        in_specs=placed,
        out_specs=(
            P(None, "dp", "fsdp", None),
            P("dp", "fsdp", None, None),
            P("dp", "fsdp", None, None),
        ),
        check_vma=False,
    )
```

```python
import jax
import jax.numpy as jnp
from jax import lax
from jax.experimental import pallas as pl
from jax.experimental.pallas import tpu as pltpu
from jax.sharding import PartitionSpec as P

MESH = pl.DeviceIdType.MESH
DECAY = 0.95
BR, BCD, ROWS, B = 16, 7, 8, 256
NBG, SLOTS, NF, NY, NDP = 112, 6, 32, 4, 8
HALF = B // 2
HR = BR // 2
Q = 2
HQ = HR // Q
LEAD = 2


def kernel(
    pg, owners, lroot, rroot, lstat, rstat,
    upd, nl, nr,
    far, raw, com, mix, near, mine, part, zout, zin_a, zin_b, snd, rcv, ret, back, table, inv, own,
    lv, rv, lsv, rsv, nlv, nrv,
    far_s, far_r, raw_s, raw_r, com_s, com_r, near_s, mine_s, z_s, z_r,
    a_s, a_r, b_s, b_r, load_s, out_s, table_s, own_s,
):
    zin = (zin_a, zin_b)
    dp = lax.axis_index("dp")
    me = lax.axis_index("fsdp")
    zh, y = dp // NY, dp % NY
    up, down = (y + 1) % NY, (y + 3) % NY
    over = (y + 2) % NY
    to = (zh * NY + up, zh * NY + down)
    across = (1 - zh) * NY + y

    barrier = pltpu.get_barrier_semaphore()
    for d in to + (across,):
        pl.semaphore_signal(barrier, inc=1, device_id={"dp": d}, device_id_type=MESH)
    for k in range(1, NF):
        pl.semaphore_signal(
            barrier, inc=1, device_id={"fsdp": (me + k) % NF}, device_id_type=MESH
        )

    def cut(c, h, rows, target):
        side = 1 - zh if h == 0 else zh
        g = side * NY + target
        return pg.at[rows, pl.ds(g * BCD, BCD), :, pl.ds(c * HALF, HALF)]

    own_cp = pltpu.make_async_copy(owners, own, own_s)
    own_cp.start()

    units = [(c, h, q) for h in range(2) for c in range(2) for q in range(Q)]
    n_units = len(units)

    def rows(q, d):
        return pl.ds(d * HR + q * HQ, HQ)

    near_cp, mine_cp = {}, {}
    for u, (c, h, q) in enumerate(units):
        for d, target in enumerate((up, down)):
            near_cp[u, d] = pltpu.make_async_copy(
                cut(c, h, rows(q, d), target), near.at[u, d], near_s.at[u, d]
            )
            near_cp[u, d].start()
            mine_cp[u, d] = pltpu.make_async_copy(
                cut(c, h, rows(q, d), y), mine.at[u, d], mine_s.at[u, d]
            )
            mine_cp[u, d].start()
    loads = [
        pltpu.make_async_copy(src, dst, load_s.at[i])
        for i, (src, dst) in enumerate(((lroot, lv), (rroot, rv), (lstat, lsv), (rstat, rsv)))
    ]

    pl.semaphore_wait(barrier, 3 + NF - 1)

    def remote(src, dst, s, r, device):
        cp = pltpu.make_async_remote_copy(
            src_ref=src, dst_ref=dst, send_sem=s, recv_sem=r, device_id=device, device_id_type=MESH
        )
        cp.start()
        return cp

    far_cp, raw_cp, com_cp, z_cp = {}, {}, {}, {}

    def send_far(u):
        if u >= n_units:
            return
        c, h, q = units[u]
        for d in range(2):
            far_cp[u, d] = remote(
                cut(c, h, rows(q, d), over), far.at[u, d], far_s.at[u, d], far_r.at[u, d],
                {"dp": to[d]},
            )

    def send_raw(u):
        if u >= n_units:
            return
        c, h, q = units[u]
        for d, target in enumerate((up, down)):
            raw_cp[u, d] = remote(
                cut(c, h, rows(q, 1 - d), target), raw.at[u, d], raw_s.at[u, d], raw_r.at[u, d],
                {"dp": to[d]},
            )

    def send_com(u):
        for d in range(2):
            near_cp[u, d].wait()
            far_cp[u, d].wait_recv()

            def add(i, _):
                mix[u, d, i] = far[u, d, i] + near[u, d, i]
                return 0

            lax.fori_loop(0, HQ, add, 0)
            com_cp[u, d] = remote(
                mix.at[u, d], com.at[u, d], com_s.at[u, d], com_r.at[u, d], {"dp": to[d]}
            )

    def finish(u):
        c, h, q = units[u]
        for d in range(2):
            mine_cp[u, d].wait()
            raw_cp[u, d].wait_recv()
            com_cp[u, d].wait_recv()
        f32 = jnp.float32

        def add(i, _):
            for d in range(2):
                total = mine[u, d, i].astype(f32) + com[u, d, i].astype(f32)
                total = total + raw[u, 1 - d, i].astype(f32)
                at = pl.ds(((q * 2 + d) * HQ + i) * BCD, BCD)
                if h == 0:
                    zout[c, at] = total.astype(jnp.bfloat16)
                else:
                    part[c, at] = total
            return 0

        lax.fori_loop(0, HQ, add, 0)
        if h == 0:
            at = pl.ds(q * (NBG // Q), NBG // Q)
            z_cp[c, q] = remote(
                zout.at[c, at], zin[c].at[at], z_s.at[c, q], z_r.at[c, q], {"dp": across}
            )

    def owner_copy(c, k):
        dst = (me + k) % NF
        return pltpu.make_async_remote_copy(
            src_ref=snd.at[c, pl.ds(dst * SLOTS, SLOTS)], dst_ref=rcv.at[c, me],
            send_sem=a_s.at[c, k], recv_sem=a_r.at[c, k],
            device_id={"fsdp": dst}, device_id_type=MESH,
        )

    def return_copy(p, k):
        dst = (me + k) % NF
        return pltpu.make_async_remote_copy(
            src_ref=ret.at[dst, pl.ds(2 * p, 2)], dst_ref=back.at[pl.ds(me * SLOTS + 2 * p, 2)],
            send_sem=b_s.at[p, k], recv_sem=b_r.at[p, k],
            device_id={"fsdp": dst}, device_id_type=MESH,
        )

    def each(act):
        def go(k, _):
            act(k)
            return 0

        lax.fori_loop(1, NF, go, 0)

    def pack(c, dst):
        for j in range(SLOTS):
            e = jnp.maximum(inv[dst, j], 0)
            total = (part[c, e] + zin[c][e].astype(jnp.float32)) * (1.0 / NDP)
            snd[c, dst * SLOTS + j] = total.astype(jnp.bfloat16)

    def exchange(c):
        for q in range(Q):
            z_cp[c, q].wait_recv()

        def go(k):
            pack(c, (me + k) % NF)
            owner_copy(c, k).start()

        each(go)
        pack(c, me)
        rcv[c, me] = snd[c, pl.ds(me * SLOTS, SLOTS)]

    for u in range(LEAD):
        send_far(u)
    send_raw(0)

    own_cp.wait()
    lane = lax.broadcasted_iota(jnp.int32, (NF, 128), 1)
    slot = lax.broadcasted_iota(jnp.int32, (NF, 128), 0) * SLOTS + lane
    slot = jnp.where(lane < SLOTS, slot, -1)

    def enter(r, held):
        d, q, i = r // HR, r % HR // HQ, r % HQ
        first = ((q * 2 + d) * HQ + i) * BCD
        for b in range(BCD):
            held = jnp.where(slot == own[r, dp * BCD + b], first + b, held)
        return held

    table[...] = lax.fori_loop(0, BR, enter, jnp.full((NF, 128), -1, jnp.int32))
    table_cp = pltpu.make_async_copy(table, inv, table_s)
    table_cp.start()

    for u in range(n_units):
        send_com(u)
        send_far(u + LEAD)
        send_raw(u + 1)
        if u == LEAD:
            for cp in loads:
                cp.start()
        if u >= 1:
            finish(u - 1)
        if u - 1 == 3 * Q - 1:
            table_cp.wait()
            exchange(0)
    finish(n_units - 1)
    exchange(1)

    for c in range(2):
        each(lambda k: owner_copy(c, k).wait_recv())
    for cp in loads:
        cp.wait()

    def block(s):
        halves = [
            rcv[c, :, s].astype(jnp.float32).reshape(B, HALF).astype(jnp.bfloat16) for c in range(2)
        ]
        return jnp.concatenate(halves, axis=1)

    def work(p, _):
        for j in range(2):
            s = 2 * p + j
            g = block(s)
            half = jnp.dot(lv[s], g, preferred_element_type=jnp.float32).astype(jnp.bfloat16)
            u = jnp.dot(half, rv[s], preferred_element_type=jnp.float32).astype(jnp.bfloat16)
            ret[:, s] = u.astype(jnp.float32).reshape(NF, ROWS, B).astype(jnp.bfloat16)
        each(lambda k: return_copy(p, k).start())
        back[pl.ds(me * SLOTS + 2 * p, 2)] = ret[me, pl.ds(2 * p, 2)]
        return 0

    lax.fori_loop(0, SLOTS // 2, work, 0)

    def out_copies(s):
        return [
            pltpu.make_async_copy(nlv.at[s], nl.at[s], out_s.at[0, s]),
            pltpu.make_async_copy(nrv.at[s], nr.at[s], out_s.at[1, s]),
        ]

    def statistics(s, _):
        g = block(s)
        held = inv[me, s] >= 0
        keep = jnp.where(held, jnp.float32(DECAY), jnp.float32(1.0))
        gain = jnp.where(held, jnp.float32(1.0 - DECAY), jnp.float32(0.0))
        left = lax.dot_general(g, g, (((1,), (1,)), ((), ())), preferred_element_type=jnp.float32)
        nlv[s] = keep * lsv[s] + gain * left
        right = lax.dot_general(g, g, (((0,), (0,)), ((), ())), preferred_element_type=jnp.float32)
        nrv[s] = keep * rsv[s] + gain * right
        for cp in out_copies(s):
            cp.start()
        return 0

    lax.fori_loop(0, SLOTS, statistics, 0)

    for u in range(n_units):
        for d in range(2):
            far_cp[u, d].wait_send()
            raw_cp[u, d].wait_send()
            com_cp[u, d].wait_send()
    for c in range(2):
        for q in range(Q):
            z_cp[c, q].wait_send()
        each(lambda k: owner_copy(c, k).wait_send())
    for s in range(SLOTS):
        for cp in out_copies(s):
            cp.wait()
    for p in range(SLOTS // 2):
        each(lambda k: return_copy(p, k).wait())

    def unpack(i, _):
        for j in range(BCD):
            upd[i, j] = back[own[i, dp * BCD + j]]
        return 0

    lax.fori_loop(0, BR, unpack, 0)


def body(partial_grads, owners, left_roots, right_roots, left_stats, right_stats):
    bf, f32 = jnp.bfloat16, jnp.float32
    any_ = pl.BlockSpec(memory_space=pl.ANY)
    hbm = pl.BlockSpec(memory_space=pltpu.HBM)
    vmem = pl.BlockSpec(memory_space=pltpu.VMEM)
    dma = pltpu.SemaphoreType.DMA
    unit = (4 * Q, 2, HQ, BCD, ROWS, HALF)
    piece = (2, NBG, ROWS, HALF)
    pair = (4 * Q, 2)
    upd, nl, nr = pl.pallas_call(
        kernel,
        out_shape=(
            jax.ShapeDtypeStruct((BR, BCD, ROWS, B), bf),
            jax.ShapeDtypeStruct((SLOTS, B, B), f32),
            jax.ShapeDtypeStruct((SLOTS, B, B), f32),
        ),
        in_specs=[hbm, hbm, hbm, hbm, hbm, hbm],
        out_specs=(vmem, any_, any_),
        scratch_shapes=[
            pltpu.VMEM(unit, bf), pltpu.VMEM(unit, bf), pltpu.VMEM(unit, bf), pltpu.VMEM(unit, bf),
            pltpu.VMEM(unit, bf),
            pltpu.VMEM(unit, bf),
            pltpu.VMEM(piece, f32), pltpu.VMEM(piece, bf),
            pltpu.VMEM(piece[1:], bf), pltpu.VMEM(piece[1:], bf),
            pltpu.VMEM((2, NF * SLOTS, ROWS, HALF), bf),
            pltpu.VMEM((2, NF, SLOTS, ROWS, HALF), bf),
            pltpu.VMEM((NF, SLOTS, ROWS, B), bf),
            pltpu.VMEM((NF * SLOTS, ROWS, B), bf),
            pltpu.VMEM((NF, 128), jnp.int32), pltpu.SMEM((NF, 128), jnp.int32),
            pltpu.SMEM((BR, BCD * NDP), jnp.int32),
            pltpu.VMEM((SLOTS, B, B), bf), pltpu.VMEM((SLOTS, B, B), bf),
            pltpu.VMEM((SLOTS, B, B), f32), pltpu.VMEM((SLOTS, B, B), f32),
            pltpu.VMEM((SLOTS, B, B), f32), pltpu.VMEM((SLOTS, B, B), f32),
            dma(pair), dma(pair), dma(pair), dma(pair), dma(pair), dma(pair),
            dma(pair), dma(pair), dma((2, Q)), dma((2, Q)),
            dma((2, NF)), dma((2, NF)), dma((3, NF)), dma((3, NF)), dma((4,)), dma((2, SLOTS)), dma, dma,
        ],
        compiler_params=pltpu.CompilerParams(
            collective_id=0, has_side_effects=True, vmem_limit_bytes=48 * 2**20
        ),
        name="step",
    )(
        partial_grads[0],
        *(
            pltpu.with_memory_space_constraint(x[0], pltpu.HBM)
            for x in (owners[None], left_roots, right_roots, left_stats, right_stats)
        ),
    )
    return upd, nl[None], nr[None]


def solution(mesh):
    placed = (
        P("dp", None, None, "fsdp", None),
        P(),
        P("dp", "fsdp", None, None),
        P("dp", "fsdp", None, None),
        P("dp", "fsdp", None, None),
        P("dp", "fsdp", None, None),
    )
    return jax.shard_map(
        body,
        mesh=mesh,
        in_specs=placed,
        out_specs=(
            P(None, "dp", "fsdp", None),
            P("dp", "fsdp", None, None),
            P("dp", "fsdp", None, None),
        ),
        check_vma=False,
    )
```

```python
import jax
import jax.numpy as jnp
from jax import lax
from jax.experimental import pallas as pl
from jax.experimental.pallas import tpu as pltpu
from jax.sharding import PartitionSpec as P

MESH = pl.DeviceIdType.MESH
DECAY = 0.95
BR, BCD, ROWS, B = 16, 7, 8, 256
NBG, SLOTS, NF, NY, NDP = 112, 6, 32, 4, 8
HALF = B // 2
HR = BR // 2
Q = 2
HQ = HR // Q
LEAD = 2


def kernel(
    pg, owners, lroot, rroot, lstat, rstat,
    upd, nl, nr,
    far, raw, com, mix, near, mine, part, zout, zin_a, zin_b, snd, rcv, ret, back, table, inv, own,
    lv, rv, lsv, rsv, nlv, nrv,
    far_s, far_r, raw_s, raw_r, com_s, com_r, near_s, mine_s, z_s, z_r,
    a_s, a_r, b_s, b_r, load_s, out_s, table_s, own_s, ready,
):
    zin = (zin_a, zin_b)
    dp = lax.axis_index("dp")
    me = lax.axis_index("fsdp")
    zh, y = dp // NY, dp % NY
    up, down = (y + 1) % NY, (y + 3) % NY
    over = (y + 2) % NY
    to = (zh * NY + up, zh * NY + down)
    across = (1 - zh) * NY + y

    barrier = pltpu.get_barrier_semaphore()
    for d in to + (across,):
        pl.semaphore_signal(barrier, inc=1, device_id={"dp": d}, device_id_type=MESH)
    bits = [1 << b for b in range(NF.bit_length() - 1)]
    mates = [me + bit * (1 - 2 * (me // bit % 2)) for bit in bits]
    for mate in mates:
        pl.semaphore_signal(barrier, inc=1, device_id={"fsdp": mate}, device_id_type=MESH)

    def cut(c, h, rows, target):
        side = 1 - zh if h == 0 else zh
        g = side * NY + target
        return pg.at[rows, pl.ds(g * BCD, BCD), :, pl.ds(c * HALF, HALF)]

    own_cp = pltpu.make_async_copy(owners, own, own_s)
    own_cp.start()

    units = [(c, h, q) for h in range(2) for c in range(2) for q in range(Q)]
    n_units = len(units)

    def rows(q, d):
        return pl.ds(d * HR + q * HQ, HQ)

    near_cp, mine_cp = {}, {}
    for u, (c, h, q) in enumerate(units):
        for d, target in enumerate((up, down)):
            near_cp[u, d] = pltpu.make_async_copy(
                cut(c, h, rows(q, d), target), near.at[u, d], near_s.at[u, d]
            )
            near_cp[u, d].start()
            mine_cp[u, d] = pltpu.make_async_copy(
                cut(c, h, rows(q, d), y), mine.at[u, d], mine_s.at[u, d]
            )
            mine_cp[u, d].start()
    loads = [
        pltpu.make_async_copy(src, dst, load_s.at[i])
        for i, (src, dst) in enumerate(((lroot, lv), (rroot, rv), (lstat, lsv), (rstat, rsv)))
    ]

    pl.semaphore_wait(barrier, 3 + len(mates))

    def remote(src, dst, s, r, device):
        cp = pltpu.make_async_remote_copy(
            src_ref=src, dst_ref=dst, send_sem=s, recv_sem=r, device_id=device, device_id_type=MESH
        )
        cp.start()
        return cp

    far_cp, raw_cp, com_cp, z_cp = {}, {}, {}, {}

    def send_far(u):
        if u >= n_units:
            return
        c, h, q = units[u]
        for d in range(2):
            far_cp[u, d] = remote(
                cut(c, h, rows(q, d), over), far.at[u, d], far_s.at[u, d], far_r.at[u, d],
                {"dp": to[d]},
            )

    def send_raw(u):
        if u >= n_units:
            return
        c, h, q = units[u]
        for d, target in enumerate((up, down)):
            raw_cp[u, d] = remote(
                cut(c, h, rows(q, 1 - d), target), raw.at[u, d], raw_s.at[u, d], raw_r.at[u, d],
                {"dp": to[d]},
            )

    def send_com(u):
        for d in range(2):
            near_cp[u, d].wait()
            far_cp[u, d].wait_recv()

            def add(i, _):
                mix[u, d, i] = far[u, d, i] + near[u, d, i]
                return 0

            lax.fori_loop(0, HQ, add, 0)
            com_cp[u, d] = remote(
                mix.at[u, d], com.at[u, d], com_s.at[u, d], com_r.at[u, d], {"dp": to[d]}
            )

    def finish(u):
        c, h, q = units[u]
        for d in range(2):
            mine_cp[u, d].wait()
            raw_cp[u, d].wait_recv()
            com_cp[u, d].wait_recv()
        f32 = jnp.float32

        def add(i, _):
            for d in range(2):
                total = mine[u, d, i].astype(f32) + com[u, d, i].astype(f32)
                total = total + raw[u, 1 - d, i].astype(f32)
                at = pl.ds(((q * 2 + d) * HQ + i) * BCD, BCD)
                if h == 0:
                    zout[c, at] = total.astype(jnp.bfloat16)
                else:
                    part[c, at] = total
            return 0

        lax.fori_loop(0, HQ, add, 0)
        if h == 0:
            at = pl.ds(q * (NBG // Q), NBG // Q)
            z_cp[c, q] = remote(
                zout.at[c, at], zin[c].at[at], z_s.at[c, q], z_r.at[c, q], {"dp": across}
            )

    def owner_copy(c, k):
        dst = (me + k) % NF
        return pltpu.make_async_remote_copy(
            src_ref=snd.at[c, pl.ds(dst * SLOTS, SLOTS)], dst_ref=rcv.at[c, me],
            send_sem=a_s.at[c, k], recv_sem=a_r.at[c, k],
            device_id={"fsdp": dst}, device_id_type=MESH,
        )

    def return_copy(p, k):
        dst = (me + k) % NF
        return pltpu.make_async_remote_copy(
            src_ref=ret.at[dst, pl.ds(6 * p, 6)], dst_ref=back.at[pl.ds(me * SLOTS + 6 * p, 6)],
            send_sem=b_s.at[p, k], recv_sem=b_r.at[p, k],
            device_id={"fsdp": dst}, device_id_type=MESH,
        )

    def each(act):
        def go(k, _):
            act(k)
            return 0

        lax.fori_loop(1, NF, go, 0)

    def pack(c, dst):
        for j in range(SLOTS):
            e = jnp.maximum(inv[dst, j], 0)
            total = (part[c, e] + zin[c][e].astype(jnp.float32)) * (1.0 / NDP)
            snd[c, dst * SLOTS + j] = total.astype(jnp.bfloat16)

    def exchange(c):
        for q in range(Q):
            z_cp[c, q].wait_recv()

        def go(k):
            pack(c, (me + k) % NF)
            owner_copy(c, k).start()

        each(go)
        pack(c, me)
        rcv[c, me] = snd[c, pl.ds(me * SLOTS, SLOTS)]

    for u in range(LEAD):
        send_far(u)
    send_raw(0)

    own_cp.wait()
    lane = lax.broadcasted_iota(jnp.int32, (NF, 128), 1)
    slot = lax.broadcasted_iota(jnp.int32, (NF, 128), 0) * SLOTS + lane
    slot = jnp.where(lane < SLOTS, slot, -1)

    def enter(r, held):
        d, q, i = r // HR, r % HR // HQ, r % HQ
        first = ((q * 2 + d) * HQ + i) * BCD
        for b in range(BCD):
            held = jnp.where(slot == own[r, dp * BCD + b], first + b, held)
        return held

    table[...] = lax.fori_loop(0, BR, enter, jnp.full((NF, 128), -1, jnp.int32))
    table_cp = pltpu.make_async_copy(table, inv, table_s)
    table_cp.start()

    def greet(b):
        pl.semaphore_signal(ready.at[b], inc=1, device_id={"fsdp": mates[b]}, device_id_type=MESH)

    greet(1)
    for u in range(n_units):
        if 0 < u < len(mates):
            pl.semaphore_wait(ready.at[u], 1)
            if u + 1 < len(mates):
                greet(u + 1)
        send_com(u)
        send_far(u + LEAD)
        send_raw(u + 1)
        if u == LEAD:
            for cp in loads:
                cp.start()
        if u >= 1:
            finish(u - 1)
        if u - 1 == 3 * Q - 1:
            table_cp.wait()
            exchange(0)
    finish(n_units - 1)
    exchange(1)

    for c in range(2):
        each(lambda k: owner_copy(c, k).wait_recv())
    for cp in loads:
        cp.wait()

    def block(s):
        halves = [
            rcv[c, :, s].astype(jnp.float32).reshape(B, HALF).astype(jnp.bfloat16) for c in range(2)
        ]
        return jnp.concatenate(halves, axis=1)

    def work(p, _):
        for j in range(6):
            s = 6 * p + j
            g = block(s)
            half = jnp.dot(lv[s], g, preferred_element_type=jnp.float32).astype(jnp.bfloat16)
            u = jnp.dot(half, rv[s], preferred_element_type=jnp.float32).astype(jnp.bfloat16)
            ret[:, s] = u.astype(jnp.float32).reshape(NF, ROWS, B).astype(jnp.bfloat16)
        each(lambda k: return_copy(p, k).start())
        back[pl.ds(me * SLOTS + 6 * p, 6)] = ret[me, pl.ds(6 * p, 6)]
        return 0

    lax.fori_loop(0, SLOTS // 6, work, 0)

    def out_copies(s):
        return [
            pltpu.make_async_copy(nlv.at[s], nl.at[s], out_s.at[0, s]),
            pltpu.make_async_copy(nrv.at[s], nr.at[s], out_s.at[1, s]),
        ]

    def statistics(s, _):
        g = block(s)
        held = inv[me, s] >= 0
        keep = jnp.where(held, jnp.float32(DECAY), jnp.float32(1.0))
        gain = jnp.where(held, jnp.float32(1.0 - DECAY), jnp.float32(0.0))
        left = lax.dot_general(g, g, (((1,), (1,)), ((), ())), preferred_element_type=jnp.float32)
        nlv[s] = keep * lsv[s] + gain * left
        right = lax.dot_general(g, g, (((0,), (0,)), ((), ())), preferred_element_type=jnp.float32)
        nrv[s] = keep * rsv[s] + gain * right
        for cp in out_copies(s):
            cp.start()
        return 0

    lax.fori_loop(0, SLOTS, statistics, 0)

    for u in range(n_units):
        for d in range(2):
            far_cp[u, d].wait_send()
            raw_cp[u, d].wait_send()
            com_cp[u, d].wait_send()
    for c in range(2):
        for q in range(Q):
            z_cp[c, q].wait_send()
        each(lambda k: owner_copy(c, k).wait_send())
    for s in range(SLOTS):
        for cp in out_copies(s):
            cp.wait()
    for p in range(SLOTS // 6):
        each(lambda k: return_copy(p, k).wait())

    def unpack(i, _):
        for j in range(BCD):
            upd[i, j] = back[own[i, dp * BCD + j]]
        return 0

    lax.fori_loop(0, BR, unpack, 0)


def body(partial_grads, owners, left_roots, right_roots, left_stats, right_stats):
    bf, f32 = jnp.bfloat16, jnp.float32
    any_ = pl.BlockSpec(memory_space=pl.ANY)
    hbm = pl.BlockSpec(memory_space=pltpu.HBM)
    vmem = pl.BlockSpec(memory_space=pltpu.VMEM)
    dma = pltpu.SemaphoreType.DMA
    unit = (4 * Q, 2, HQ, BCD, ROWS, HALF)
    piece = (2, NBG, ROWS, HALF)
    pair = (4 * Q, 2)
    upd, nl, nr = pl.pallas_call(
        kernel,
        out_shape=(
            jax.ShapeDtypeStruct((BR, BCD, ROWS, B), bf),
            jax.ShapeDtypeStruct((SLOTS, B, B), f32),
            jax.ShapeDtypeStruct((SLOTS, B, B), f32),
        ),
        in_specs=[hbm, hbm, hbm, hbm, hbm, hbm],
        out_specs=(vmem, any_, any_),
        scratch_shapes=[
            pltpu.VMEM(unit, bf), pltpu.VMEM(unit, bf), pltpu.VMEM(unit, bf), pltpu.VMEM(unit, bf),
            pltpu.VMEM(unit, bf),
            pltpu.VMEM(unit, bf),
            pltpu.VMEM(piece, f32), pltpu.VMEM(piece, bf),
            pltpu.VMEM(piece[1:], bf), pltpu.VMEM(piece[1:], bf),
            pltpu.VMEM((2, NF * SLOTS, ROWS, HALF), bf),
            pltpu.VMEM((2, NF, SLOTS, ROWS, HALF), bf),
            pltpu.VMEM((NF, SLOTS, ROWS, B), bf),
            pltpu.VMEM((NF * SLOTS, ROWS, B), bf),
            pltpu.VMEM((NF, 128), jnp.int32), pltpu.SMEM((NF, 128), jnp.int32),
            pltpu.SMEM((BR, BCD * NDP), jnp.int32),
            pltpu.VMEM((SLOTS, B, B), bf), pltpu.VMEM((SLOTS, B, B), bf),
            pltpu.VMEM((SLOTS, B, B), f32), pltpu.VMEM((SLOTS, B, B), f32),
            pltpu.VMEM((SLOTS, B, B), f32), pltpu.VMEM((SLOTS, B, B), f32),
            dma(pair), dma(pair), dma(pair), dma(pair), dma(pair), dma(pair),
            dma(pair), dma(pair), dma((2, Q)), dma((2, Q)),
            dma((2, NF)), dma((2, NF)), dma((3, NF)), dma((3, NF)), dma((4,)), dma((2, SLOTS)), dma, dma,
            pltpu.SemaphoreType.REGULAR((5,)),
        ],
        compiler_params=pltpu.CompilerParams(
            collective_id=0, has_side_effects=True, vmem_limit_bytes=48 * 2**20
        ),
        name="step",
    )(
        partial_grads[0],
        *(
            pltpu.with_memory_space_constraint(x[0], pltpu.HBM)
            for x in (owners[None], left_roots, right_roots, left_stats, right_stats)
        ),
    )
    return upd, nl[None], nr[None]


def solution(mesh):
    placed = (
        P("dp", None, None, "fsdp", None),
        P(),
        P("dp", "fsdp", None, None),
        P("dp", "fsdp", None, None),
        P("dp", "fsdp", None, None),
        P("dp", "fsdp", None, None),
    )
    return jax.shard_map(
        body,
        mesh=mesh,
        in_specs=placed,
        out_specs=(
            P(None, "dp", "fsdp", None),
            P("dp", "fsdp", None, None),
            P("dp", "fsdp", None, None),
        ),
        check_vma=False,
    )
```

```python
import jax
import jax.numpy as jnp
from jax import lax
from jax.experimental import pallas as pl
from jax.experimental.pallas import tpu as pltpu
from jax.sharding import PartitionSpec as P

MESH = pl.DeviceIdType.MESH
DECAY = 0.95
BR, BCD, ROWS, B = 16, 7, 8, 256
NBG, SLOTS, NF, NY, NDP = 112, 6, 32, 4, 8
HALF = B // 2
HR = BR // 2
Q = 2
HQ = HR // Q
LEAD = 2


def kernel(
    pg, owners, lroot, rroot, lstat, rstat,
    upd, nl, nr,
    far, raw, com, mix, near, mine, part, zout, zin_a, zin_b, snd, rcv, ret, back, table, inv, own,
    lv, rv, lsv, rsv, nlv, nrv,
    far_s, far_r, raw_s, raw_r, com_s, com_r, near_s, mine_s, z_s, z_r,
    a_s, a_r, b_s, b_r, load_s, out_s, table_s, own_s, ready,
):
    zin = (zin_a, zin_b)
    dp = lax.axis_index("dp")
    me = lax.axis_index("fsdp")
    zh, y = dp // NY, dp % NY
    up, down = (y + 1) % NY, (y + 3) % NY
    over = (y + 2) % NY
    to = (zh * NY + up, zh * NY + down)
    across = (1 - zh) * NY + y

    barrier = pltpu.get_barrier_semaphore()
    for d in to + (across,):
        pl.semaphore_signal(barrier, inc=1, device_id={"dp": d}, device_id_type=MESH)
    bits = [1 << b for b in range(NF.bit_length() - 1)]
    mates = [me + bit * (1 - 2 * (me // bit % 2)) for bit in bits]
    for mate in mates:
        pl.semaphore_signal(barrier, inc=1, device_id={"fsdp": mate}, device_id_type=MESH)

    def cut(c, h, rows, target):
        side = 1 - zh if h == 0 else zh
        g = side * NY + target
        return pg.at[rows, pl.ds(g * BCD, BCD), :, pl.ds(c * HALF, HALF)]

    own_cp = pltpu.make_async_copy(owners, own, own_s)
    own_cp.start()

    units = [(c, h, q) for h in range(2) for c in range(2) for q in range(Q)]
    n_units = len(units)

    def rows(q, d):
        return pl.ds(d * HR + q * HQ, HQ)

    near_cp, mine_cp = {}, {}
    for u, (c, h, q) in enumerate(units):
        for d, target in enumerate((up, down)):
            near_cp[u, d] = pltpu.make_async_copy(
                cut(c, h, rows(q, d), target), near.at[u, d], near_s.at[u, d]
            )
            near_cp[u, d].start()
            mine_cp[u, d] = pltpu.make_async_copy(
                cut(c, h, rows(q, d), y), mine.at[u, d], mine_s.at[u, d]
            )
            mine_cp[u, d].start()
    loads = [
        pltpu.make_async_copy(src, dst, load_s.at[i])
        for i, (src, dst) in enumerate(((lroot, lv), (rroot, rv), (lstat, lsv), (rstat, rsv)))
    ]

    pl.semaphore_wait(barrier, 3 + len(mates))

    def remote(src, dst, s, r, device):
        cp = pltpu.make_async_remote_copy(
            src_ref=src, dst_ref=dst, send_sem=s, recv_sem=r, device_id=device, device_id_type=MESH
        )
        cp.start()
        return cp

    far_cp, raw_cp, com_cp, z_cp = {}, {}, {}, {}

    def send_far(u):
        if u >= n_units:
            return
        c, h, q = units[u]
        for d in range(2):
            far_cp[u, d] = remote(
                cut(c, h, rows(q, d), over), far.at[u, d], far_s.at[u, d], far_r.at[u, d],
                {"dp": to[d]},
            )

    def send_raw(u):
        if u >= n_units:
            return
        c, h, q = units[u]
        for d, target in enumerate((up, down)):
            raw_cp[u, d] = remote(
                cut(c, h, rows(q, 1 - d), target), raw.at[u, d], raw_s.at[u, d], raw_r.at[u, d],
                {"dp": to[d]},
            )

    def send_com(u):
        for d in range(2):
            near_cp[u, d].wait()
            far_cp[u, d].wait_recv()

            def add(i, _):
                mix[u, d, i] = far[u, d, i] + near[u, d, i]
                return 0

            lax.fori_loop(0, HQ, add, 0)
            com_cp[u, d] = remote(
                mix.at[u, d], com.at[u, d], com_s.at[u, d], com_r.at[u, d], {"dp": to[d]}
            )

    def finish(u):
        c, h, q = units[u]
        for d in range(2):
            mine_cp[u, d].wait()
            raw_cp[u, d].wait_recv()
            com_cp[u, d].wait_recv()
        f32 = jnp.float32

        def add(i, _):
            for d in range(2):
                total = mine[u, d, i].astype(f32) + com[u, d, i].astype(f32)
                total = total + raw[u, 1 - d, i].astype(f32)
                at = pl.ds(((q * 2 + d) * HQ + i) * BCD, BCD)
                if h == 0:
                    zout[c, at] = total.astype(jnp.bfloat16)
                else:
                    part[c, at] = total
            return 0

        lax.fori_loop(0, HQ, add, 0)
        if h == 0:
            at = pl.ds(q * (NBG // Q), NBG // Q)
            z_cp[c, q] = remote(
                zout.at[c, at], zin[c].at[at], z_s.at[c, q], z_r.at[c, q], {"dp": across}
            )

    def owner_copy(c, k):
        dst = (me + k) % NF
        return pltpu.make_async_remote_copy(
            src_ref=snd.at[c, pl.ds(dst * SLOTS, SLOTS)], dst_ref=rcv.at[c, me],
            send_sem=a_s.at[c, k], recv_sem=a_r.at[c, k],
            device_id={"fsdp": dst}, device_id_type=MESH,
        )

    def return_copy(p, k):
        dst = (me + k) % NF
        return pltpu.make_async_remote_copy(
            src_ref=ret.at[dst, pl.ds(6 * p, 6)], dst_ref=back.at[pl.ds(me * SLOTS + 6 * p, 6)],
            send_sem=b_s.at[p, k], recv_sem=b_r.at[p, k],
            device_id={"fsdp": dst}, device_id_type=MESH,
        )

    def each(act):
        def go(k, _):
            act(k)
            return 0

        lax.fori_loop(1, NF, go, 0)

    def pack(c, dst):
        for j in range(SLOTS):
            e = jnp.maximum(inv[dst, j], 0)
            total = (part[c, e] + zin[c][e].astype(jnp.float32)) * (1.0 / NDP)
            snd[c, dst * SLOTS + j] = total.astype(jnp.bfloat16)

    def exchange(c):
        for q in range(Q):
            z_cp[c, q].wait_recv()

        def go(k):
            pack(c, (me + k) % NF)
            owner_copy(c, k).start()

        each(go)
        pack(c, me)
        rcv[c, me] = snd[c, pl.ds(me * SLOTS, SLOTS)]

    for u in range(LEAD):
        send_far(u)
    send_raw(0)

    own_cp.wait()
    lane = lax.broadcasted_iota(jnp.int32, (NF, 128), 1)
    slot = lax.broadcasted_iota(jnp.int32, (NF, 128), 0) * SLOTS + lane
    slot = jnp.where(lane < SLOTS, slot, -1)

    def enter(r, held):
        d, q, i = r // HR, r % HR // HQ, r % HQ
        first = ((q * 2 + d) * HQ + i) * BCD
        for b in range(BCD):
            held = jnp.where(slot == own[r, dp * BCD + b], first + b, held)
        return held

    table[...] = lax.fori_loop(0, BR, enter, jnp.full((NF, 128), -1, jnp.int32))
    table_cp = pltpu.make_async_copy(table, inv, table_s)
    table_cp.start()

    def greet(b):
        pl.semaphore_signal(ready.at[b], inc=1, device_id={"fsdp": mates[b]}, device_id_type=MESH)

    greet(1)
    for u in range(n_units):
        if 0 < u < len(mates):
            pl.semaphore_wait(ready.at[u], 1)
            if u + 1 < len(mates):
                greet(u + 1)
        send_com(u)
        send_raw(u + 1)
        send_far(u + LEAD)
        if u == LEAD:
            for cp in loads:
                cp.start()
        if u >= 1:
            finish(u - 1)
        if u - 1 == 3 * Q - 1:
            table_cp.wait()
            exchange(0)
    finish(n_units - 1)
    exchange(1)

    for c in range(2):
        each(lambda k: owner_copy(c, k).wait_recv())
    for cp in loads:
        cp.wait()

    def block(s):
        halves = [
            rcv[c, :, s].astype(jnp.float32).reshape(B, HALF).astype(jnp.bfloat16) for c in range(2)
        ]
        return jnp.concatenate(halves, axis=1)

    def work(p, _):
        for j in range(6):
            s = 6 * p + j
            g = block(s)
            half = jnp.dot(lv[s], g, preferred_element_type=jnp.float32).astype(jnp.bfloat16)
            u = jnp.dot(half, rv[s], preferred_element_type=jnp.float32).astype(jnp.bfloat16)
            ret[:, s] = u.astype(jnp.float32).reshape(NF, ROWS, B).astype(jnp.bfloat16)
        each(lambda k: return_copy(p, k).start())
        back[pl.ds(me * SLOTS + 6 * p, 6)] = ret[me, pl.ds(6 * p, 6)]
        return 0

    lax.fori_loop(0, SLOTS // 6, work, 0)

    def out_copies(s):
        return [
            pltpu.make_async_copy(nlv.at[s], nl.at[s], out_s.at[0, s]),
            pltpu.make_async_copy(nrv.at[s], nr.at[s], out_s.at[1, s]),
        ]

    def statistics(s, _):
        g = block(s)
        held = inv[me, s] >= 0
        keep = jnp.where(held, jnp.float32(DECAY), jnp.float32(1.0))
        gain = jnp.where(held, jnp.float32(1.0 - DECAY), jnp.float32(0.0))
        left = lax.dot_general(g, g, (((1,), (1,)), ((), ())), preferred_element_type=jnp.float32)
        nlv[s] = keep * lsv[s] + gain * left
        right = lax.dot_general(g, g, (((0,), (0,)), ((), ())), preferred_element_type=jnp.float32)
        nrv[s] = keep * rsv[s] + gain * right
        for cp in out_copies(s):
            cp.start()
        return 0

    lax.fori_loop(0, SLOTS, statistics, 0)

    for u in range(n_units):
        for d in range(2):
            far_cp[u, d].wait_send()
            raw_cp[u, d].wait_send()
            com_cp[u, d].wait_send()
    for c in range(2):
        for q in range(Q):
            z_cp[c, q].wait_send()
        each(lambda k: owner_copy(c, k).wait_send())
    for s in range(SLOTS):
        for cp in out_copies(s):
            cp.wait()
    for p in range(SLOTS // 6):
        each(lambda k: return_copy(p, k).wait())

    def unpack(i, _):
        for j in range(BCD):
            upd[i, j] = back[own[i, dp * BCD + j]]
        return 0

    lax.fori_loop(0, BR, unpack, 0)


def body(partial_grads, owners, left_roots, right_roots, left_stats, right_stats):
    bf, f32 = jnp.bfloat16, jnp.float32
    any_ = pl.BlockSpec(memory_space=pl.ANY)
    hbm = pl.BlockSpec(memory_space=pltpu.HBM)
    vmem = pl.BlockSpec(memory_space=pltpu.VMEM)
    dma = pltpu.SemaphoreType.DMA
    unit = (4 * Q, 2, HQ, BCD, ROWS, HALF)
    piece = (2, NBG, ROWS, HALF)
    pair = (4 * Q, 2)
    upd, nl, nr = pl.pallas_call(
        kernel,
        out_shape=(
            jax.ShapeDtypeStruct((BR, BCD, ROWS, B), bf),
            jax.ShapeDtypeStruct((SLOTS, B, B), f32),
            jax.ShapeDtypeStruct((SLOTS, B, B), f32),
        ),
        in_specs=[hbm, hbm, hbm, hbm, hbm, hbm],
        out_specs=(vmem, any_, any_),
        scratch_shapes=[
            pltpu.VMEM(unit, bf), pltpu.VMEM(unit, bf), pltpu.VMEM(unit, bf), pltpu.VMEM(unit, bf),
            pltpu.VMEM(unit, bf),
            pltpu.VMEM(unit, bf),
            pltpu.VMEM(piece, f32), pltpu.VMEM(piece, bf),
            pltpu.VMEM(piece[1:], bf), pltpu.VMEM(piece[1:], bf),
            pltpu.VMEM((2, NF * SLOTS, ROWS, HALF), bf),
            pltpu.VMEM((2, NF, SLOTS, ROWS, HALF), bf),
            pltpu.VMEM((NF, SLOTS, ROWS, B), bf),
            pltpu.VMEM((NF * SLOTS, ROWS, B), bf),
            pltpu.VMEM((NF, 128), jnp.int32), pltpu.SMEM((NF, 128), jnp.int32),
            pltpu.SMEM((BR, BCD * NDP), jnp.int32),
            pltpu.VMEM((SLOTS, B, B), bf), pltpu.VMEM((SLOTS, B, B), bf),
            pltpu.VMEM((SLOTS, B, B), f32), pltpu.VMEM((SLOTS, B, B), f32),
            pltpu.VMEM((SLOTS, B, B), f32), pltpu.VMEM((SLOTS, B, B), f32),
            dma(pair), dma(pair), dma(pair), dma(pair), dma(pair), dma(pair),
            dma(pair), dma(pair), dma((2, Q)), dma((2, Q)),
            dma((2, NF)), dma((2, NF)), dma((3, NF)), dma((3, NF)), dma((4,)), dma((2, SLOTS)), dma, dma,
            pltpu.SemaphoreType.REGULAR((5,)),
        ],
        compiler_params=pltpu.CompilerParams(
            collective_id=0, has_side_effects=True, vmem_limit_bytes=48 * 2**20
        ),
        name="step",
    )(
        partial_grads[0],
        *(
            pltpu.with_memory_space_constraint(x[0], pltpu.HBM)
            for x in (owners[None], left_roots, right_roots, left_stats, right_stats)
        ),
    )
    return upd, nl[None], nr[None]


def solution(mesh):
    placed = (
        P("dp", None, None, "fsdp", None),
        P(),
        P("dp", "fsdp", None, None),
        P("dp", "fsdp", None, None),
        P("dp", "fsdp", None, None),
        P("dp", "fsdp", None, None),
    )
    return jax.shard_map(
        body,
        mesh=mesh,
        in_specs=placed,
        out_specs=(
            P(None, "dp", "fsdp", None),
            P("dp", "fsdp", None, None),
            P("dp", "fsdp", None, None),
        ),
        check_vma=False,
    )
```
